512 devices in a mesh: blk: 64 (over z_hi, y, core), group: 8 (over x, z_lo).
Axes of the slice: x: 4, y: 8, z: 8 (z_hi: 4, z_lo: 2; z = z_hi * 2 + z_lo), core: 2. Of those that a mesh axis runs over, the one named last changes fastest.
Arguments:
- activations: bfloat16 [65536, 2560], P(('blk', 'group')), may hold values from -6 to 6
- grad_out: bfloat16 [65536, 8192], P(('blk', 'group')), may hold values from -0.125 to 0.125
- kept_rows: int32 [512, 128], P(('blk', 'group')), may hold values from 0 to 19, as said below
- kept_cols: int32 [512, 128], P(('blk', 'group')), may hold values from 0 to 63, as said below
- kept_count: int32 [512], P(('blk', 'group')), may hold values from 2 to 128
- owner_tiles: int32 [1280], replicated, may hold values from 0 to 1279, as said below
- apply_mask: int32 [1280], P('blk'), may hold values 0 or 1
- feedback_in: bfloat16 [1280, 128, 128], P('blk'), may hold values from -4 to 4
Outputs:
- update: bfloat16 [1280, 128, 128], P('blk')
- feedback: bfloat16 [1280, 128, 128], P('blk')
The draws below stay inside these ranges and needn't reach their ends.
Inputs may be any that keep to these rules, and one draw needn't show every extreme that they name: `kept_rows`: live entries of a worker name distinct tiles; of them at most 2 lie among the 20 tiles of any one owner (blk index p owns the tiles owner_tiles[p * 20] to owner_tiles[p * 20 + 19]). In every draw some worker has 2 tiles of every owner, and some owner has 2 tiles from every worker. Entries at kept_count and beyond are 0. `kept_cols`: as kept_rows, entry by entry. `owner_tiles`: A permutation of the tile numbers.
All inputs are finite; a program needn't handle non-finite values. No bound on the sum of `apply_mask` on one device may be relied on, other than what follows from the above.
Results may differ from the reference program's by a relative error of at most 0.0048.
Values may be sent and summed in bfloat16 or wider, within the bound.
A program may use at most 128 MiB of HBM per device.

```python
import jax
import jax.numpy as jnp
from jax import lax

DW = 2560
FW = 8192
TILE = 128
SLOT = 2
TOK_DEV = 128
TILES = 1280
TOKENS = 65536
N_BLK = 64
N_GROUP = 8


def shared_lists(key):
    key_perm, key_load, key_pick, key_order, key_full = jax.random.split(key, 5)
    tile_cols = FW // TILE
    everything = DW // TILE * tile_cols
    owned_tiles = everything // N_BLK
    workers = N_BLK * N_GROUP
    list_width = N_BLK * SLOT
    owner_tiles = jax.random.permutation(key_perm, everything).astype(jnp.int32)
    owner_loads = jax.random.randint(key_load, (workers, N_BLK), 0, SLOT + 1)
    key_worker, key_owner, key_sparse = jax.random.split(key_full, 3)
    full_worker = jax.random.randint(key_worker, (), 0, workers)
    full_owner = jax.random.randint(key_owner, (), 0, N_BLK)
    sparse_worker = (full_worker + 1 + jax.random.randint(key_sparse, (), 0, workers - 1)) % workers
    owner_loads = jnp.where(jnp.arange(workers)[:, None] == full_worker, SLOT, owner_loads)
    owner_loads = jnp.where(jnp.arange(workers)[:, None] == sparse_worker, 0, owner_loads)
    owner_loads = jnp.where(jnp.arange(N_BLK)[None, :] == full_owner, SLOT, owner_loads)
    scores = jax.random.randint(key_pick, (workers, N_BLK, owned_tiles), 0, 1 << 20) * owned_tiles + jnp.arange(owned_tiles)
    chosen = jnp.argsort(scores, axis=-1)[:, :, :SLOT]
    position = jnp.arange(N_BLK)[None, :, None] * owned_tiles + chosen
    tile_ids = owner_tiles[position].reshape(workers, list_width)
    alive_slot = (jnp.arange(SLOT)[None, None, :] < owner_loads[:, :, None]).reshape(workers, list_width)
    shuffle = jax.random.randint(key_order, (workers, list_width), 0, 1 << 20) * list_width + jnp.arange(list_width)
    sort_order = jnp.argsort(jnp.where(alive_slot, shuffle, shuffle + (1 << 29)), axis=-1)
    tile_ids = jnp.take_along_axis(tile_ids, sort_order, axis=-1)
    alive_slot = jnp.take_along_axis(alive_slot, sort_order, axis=-1)
    row_ids = jnp.where(alive_slot, tile_ids // tile_cols, 0).astype(jnp.int32)
    col_ids = jnp.where(alive_slot, tile_ids % tile_cols, 0).astype(jnp.int32)
    counts = jnp.sum(alive_slot.astype(jnp.int32), axis=-1).astype(jnp.int32)
    return (owner_tiles, row_ids, col_ids, counts)


def draw_owner_tiles(key, part):
    tables = shared_lists(key)
    return tables[0]


def draw_kept_rows(key, part):
    tables = shared_lists(key)
    return tables[1]


def draw_kept_cols(key, part):
    tables = shared_lists(key)
    return tables[2]


def draw_kept_count(key, part):
    tables = shared_lists(key)
    return tables[3]


def with_ends(array, key, least, largest):
    place = [jax.random.randint(jax.random.fold_in(key, axis), (), 0, length) for axis, length in enumerate(array.shape)]
    longest = array.shape.index(max(array.shape))
    next_to = place[:longest] + [(place[longest] + 1) % array.shape[longest]] + place[longest + 1:]
    return array.at[tuple(place)].set(least).at[tuple(next_to)].set(largest)


def block_scale(rng, dims, cuts, least, high):
    loudness = 1.0
    for dim, parts in cuts:
        heights = jax.random.uniform(jax.random.fold_in(jax.random.fold_in(rng, 6), dim), (parts,), jnp.float32, least / len(cuts), high / len(cuts))
        loudness = loudness * jnp.repeat(jnp.exp(heights), dims[dim] // parts).reshape((-1,) + (1,) * (len(dims) - 1 - dim))
    return loudness


def noise(own_key, extent, scale, bound, cuts=(), kind=jnp.bfloat16):
    level = block_scale(own_key, extent, cuts, -0.22, 0.18) if cuts else 1.0
    drawn = jax.random.normal(own_key, extent, jnp.float32) * scale * level
    return jnp.minimum(jnp.maximum(drawn, -bound), bound).astype(kind)


def setup_inputs(seed: int = 0) -> dict:
    arg_keys = jax.random.split(jax.random.key(seed), 9)
    activations = noise(arg_keys[0], (TOKENS, DW), 1.0, 6.0, ((0, 512),))
    grad_out = noise(arg_keys[1], (TOKENS, FW), (16 * TOK_DEV) ** -0.5, 0.125, ((0, 512),))
    kept_rows = draw_kept_rows(jax.random.fold_in(arg_keys[8], 71), 0)
    kept_cols = draw_kept_cols(jax.random.fold_in(arg_keys[8], 71), 0)
    kept_count = draw_kept_count(jax.random.fold_in(arg_keys[8], 71), 0)
    owner_tiles = draw_owner_tiles(jax.random.fold_in(arg_keys[8], 71), 0)
    apply_mask = with_ends((jax.random.randint(arg_keys[6], (TILES,), 0, 2) < 1).astype(jnp.int32), jax.random.fold_in(arg_keys[6], 1), 0, 1)
    feedback_in = noise(arg_keys[7], (TILES, TILE, TILE), 0.5, 4.0, ((0, 64),))
    return {"activations": activations, "grad_out": grad_out, "kept_rows": kept_rows, "kept_cols": kept_cols, "kept_count": kept_count, "owner_tiles": owner_tiles, "apply_mask": apply_mask, "feedback_in": feedback_in}


def reference(activations, grad_out, kept_rows, kept_cols, kept_count, owner_tiles, apply_mask, feedback_in):
    tile_rows = DW // TILE
    tile_cols = FW // TILE
    workers = N_BLK * N_GROUP
    act_tiles = activations.reshape(workers, TOK_DEV, tile_rows, TILE)
    grad_tiles = grad_out.reshape(workers, TOK_DEV, tile_cols, TILE)

    def add_worker(running, item):
        act_now, grad_now, row_now, col_now, count_now = item
        left_cols = jnp.take(act_now, row_now, axis=1).astype(jnp.float32)
        right_cols = jnp.take(grad_now, col_now, axis=1).astype(jnp.float32)
        product = jnp.einsum("ksa,ksb->sab", left_cols, right_cols).astype(jnp.bfloat16)
        product = lax.optimization_barrier(product).astype(jnp.float32)
        live_entry = (jnp.arange(row_now.shape[0]) < count_now).astype(jnp.float32)
        tile_ids = (row_now * tile_cols + col_now).astype(jnp.int32)
        running = running.at[tile_ids].add(product * live_entry[:, None, None])
        return running, None

    start_sum = jnp.zeros((tile_rows * tile_cols, TILE, TILE), jnp.float32)
    gradient_sum, _ = lax.scan(add_worker, start_sum, (act_tiles, grad_tiles, kept_rows, kept_cols, kept_count))
    accumulated = gradient_sum[owner_tiles] + feedback_in.astype(jnp.float32)
    applied = (apply_mask == 1)[:, None, None]
    update = jnp.where(applied, accumulated, 0.0).astype(jnp.bfloat16)
    feedback = jnp.where(applied, 0.0, accumulated).astype(jnp.bfloat16)
    return update, feedback
```

```python
import functools

import jax
import jax.numpy as jnp
from jax import lax
from jax.experimental import pallas as pl
from jax.experimental.pallas import tpu as pltpu
from jax.sharding import PartitionSpec as P

ZH, YN, CORES, XN, ZL = 4, 8, 2, 4, 2
SLICES = XN * ZL
CLUSTER = SLICES * CORES
SLOT = 2
TILE = 128
ROWS = TILE // SLICES
OWNED = 20
PIECE = OWNED * ROWS
PER_CHUNK = YN * SLOT
MESH = pl.DeviceIdType.MESH
F32 = jnp.float32
BF16 = jnp.bfloat16


def prep_kernel(count_ref, rows_ref, cols_ref, tiles_ref, table_ref, code_ref):
    n = TILE
    sub = lax.broadcasted_iota(jnp.int32, (n, n), 0).astype(F32)
    lane = lax.broadcasted_iota(jnp.int32, (n, n), 1).astype(F32)
    count = count_ref[0].astype(F32)
    row_of = jnp.broadcast_to(rows_ref[...].astype(F32), (n, n)).T
    col_of = jnp.broadcast_to(cols_ref[...].astype(F32), (n, n)).T
    tile_of = row_of * 64.0 + col_of
    found = jnp.zeros((n, n), F32)
    for k in range(tiles_ref.shape[0]):
        known = tiles_ref[k : k + 1, :].astype(F32)
        found += jnp.where(tile_of == known, lane + 128.0 * k, 0.0)
    position = jnp.broadcast_to(jnp.sum(found, axis=1, keepdims=True), (n, n))
    owner = jnp.floor((position + 0.5) * (1.0 / OWNED))
    label = position - OWNED * owner
    same = (owner.T == owner) & (lane < sub) & (lane < count)
    rank = jnp.sum(jnp.where(same, 1.0, 0.0), axis=1, keepdims=True)
    z_hi = jnp.floor((owner + 0.5) * (1.0 / 16.0))
    in_plane = owner - 16.0 * z_hi
    y = jnp.floor((in_plane + 0.5) * 0.5)
    core = in_plane - 2.0 * y
    slot = ((z_hi * 2.0 + core) * 8.0 + y) * 2.0 + rank
    chosen = (slot == lane) & (sub < count)
    slot_row = jnp.sum(jnp.where(chosen, row_of, 0.0), axis=0, keepdims=True)
    slot_col = jnp.sum(jnp.where(chosen, col_of, 0.0), axis=0, keepdims=True)
    slot_label = jnp.sum(jnp.where(chosen, label + 1.0, 0.0), axis=0, keepdims=True) - 1.0
    table_ref[0:1, :] = slot_row.astype(jnp.int32)
    table_ref[1:2, :] = slot_col.astype(jnp.int32)
    m = CORES * ZH * YN
    at = lax.broadcasted_iota(jnp.int32, (m, n), 0)
    s = lax.broadcasted_iota(jnp.int32, (m, n), 1)
    want = ((at // 8) % 4 * 2 + at // 32) * 8 + at % 8
    spread = jnp.where(s // 2 == want, jnp.broadcast_to(slot_label, (m, n)), 0.0).astype(BF16)
    s2 = lax.broadcasted_iota(jnp.int32, (n, n), 0)
    l2 = lax.broadcasted_iota(jnp.int32, (n, n), 1)
    pick = jnp.where(s2 % 2 == (l2 % 32) // 16, 1.0, 0.0).astype(BF16)
    coded = jnp.dot(spread, pick, preferred_element_type=F32) * 16.0
    coded += (lax.broadcasted_iota(jnp.int32, (m, n), 1) % 16).astype(F32)
    code_ref[...] = coded.reshape(CORES, ZH, YN, n)


def main_kernel(
    table_ref, code_ref, act_ref, grad_ref, back_ref, out_ref,
    act_t, grad_t, made, got, codes, keys, sums, to_right, from_left, to_left, from_right, to_z, from_z,
    code_send, code_recv, made_send, made_recv,
    right_send, right_recv, left_send, left_recv, z_send, z_recv, out_send, out_recv,
):
    blk = lax.axis_index("blk")
    group = lax.axis_index("group")
    z_hi, y, core = blk // 16, (blk // 2) % 8, blk % 2
    x, z_lo = group // 2, group % 2
    me = group * 2 + core

    def device(z_hi_at, y_at, core_at, group_at):
        return ((z_hi_at * 8 + y_at) * 2 + core_at, group_at)

    def peer(n, way):
        dx, dz, dc = n // 4, (n // 2) % 2, n % 2
        return ((x + way * dx + XN) % XN) * 2 + (z_lo + dz) % 2, (core + dc) % 2

    right = device(z_hi, (y + 1) % 8, core, group)
    left = device(z_hi, (y + 7) % 8, core, group)

    barrier = pltpu.get_barrier_semaphore()

    def greet(n, _):
        g, c = peer(n, 1)
        pl.semaphore_signal(barrier, inc=1, device_id=device(z_hi, y, c, g), device_id_type=MESH)
        return 0

    lax.fori_loop(1, CLUSTER, greet, 0)
    for there in (right, left):
        pl.semaphore_signal(barrier, inc=1, device_id=there, device_id_type=MESH)
    for k in range(1, ZH):
        pl.semaphore_signal(
            barrier, inc=1, device_id=device((z_hi + k) % 4, y, core, group), device_id_type=MESH
        )

    def turn(r, _):
        at = pl.ds(pl.multiple_of(r * TILE, TILE), TILE)
        act_t[r] = act_ref[:, at].T
        return 0

    lax.fori_loop(0, act_ref.shape[1] // TILE, turn, 0)

    def part(r, _):
        grad_t[r] = grad_ref[:, pl.ds(pl.multiple_of(r * TILE, TILE), TILE)]
        return 0

    lax.fori_loop(0, grad_ref.shape[1] // TILE, part, 0)

    def make(k):
        z_to = (z_hi + 1 + k) % 4

        def one(s, _):
            c, slot = s // PER_CHUNK, s % PER_CHUNK
            e = z_to * (CORES * PER_CHUNK) + s
            a, b = act_t[table_ref[0, e]], grad_t[table_ref[1, e]]
            tile = jnp.dot(a, b, preferred_element_type=F32).astype(BF16)
            made[k, c, :, slot] = tile.reshape(SLICES, ROWS, TILE)
            return 0

        lax.fori_loop(0, CORES * PER_CHUNK, one, 0, unroll=4)

    def code_copy(n, way):
        g, c = peer(n, way)
        return pltpu.make_async_remote_copy(
            src_ref=code_ref.at[c],
            dst_ref=codes.at[me if way == 1 else g * 2 + c],
            send_sem=code_send.at[n],
            recv_sem=code_recv.at[n],
            device_id=device(z_hi, y, c, g),
            device_id_type=MESH,
        )

    def made_copy(k, n, way):
        g, c = peer(n, way)
        return pltpu.make_async_remote_copy(
            src_ref=made.at[k, c, g],
            dst_ref=got.at[k, me if way == 1 else g * 2 + c],
            send_sem=made_send.at[k, n],
            recv_sem=made_recv.at[k, n],
            device_id=device(z_hi, y, c, g),
            device_id_type=MESH,
        )

    def each_peer(do):
        def step(n, _):
            do(n)
            return 0

        lax.fori_loop(1, CLUSTER, step, 0)

    make(0)
    pl.semaphore_wait(barrier, CLUSTER - 1 + 2 + ZH - 1)
    each_peer(lambda n: code_copy(n, 1).start())
    each_peer(lambda n: made_copy(0, n, 1).start())
    codes[me] = code_ref[core]
    for k in range(1, ZH):
        make(k)
        each_peer(lambda n, k=k: made_copy(k, n, 1).start())
    for k in range(ZH):
        got[k, me] = made[k, core, group]
    each_peer(lambda n: code_copy(n, -1).wait_recv())

    lane = lax.broadcasted_iota(jnp.int32, (YN, TILE), 1)
    row = lax.broadcasted_iota(jnp.int32, (PIECE, CLUSTER * SLOT * ROWS), 0).astype(F32)

    def right_copy(k, s):
        return pltpu.make_async_remote_copy(
            src_ref=to_right.at[k, s], dst_ref=from_left.at[k, s],
            send_sem=right_send.at[k, s], recv_sem=right_recv.at[k, s],
            device_id=right, device_id_type=MESH,
        )

    def left_copy(k, s):
        return pltpu.make_async_remote_copy(
            src_ref=to_left.at[k, s], dst_ref=from_right.at[k, s],
            send_sem=left_send.at[k, s], recv_sem=left_recv.at[k, s],
            device_id=left, device_id_type=MESH,
        )

    def z_copy(k):
        return pltpu.make_async_remote_copy(
            src_ref=to_z.at[k], dst_ref=from_z.at[k],
            send_sem=z_send.at[k], recv_sem=z_recv.at[k],
            device_id=device((z_hi + 1 + k) % 4, y, core, group), device_id_type=MESH,
        )

    total = None
    for k in range(ZH):
        z_to = (z_hi + 1 + k) % 4
        each_peer(lambda n, k=k: made_copy(k, n, -1).wait_recv())
        for kk in range(4):
            key = jnp.zeros((YN, TILE), F32)
            for i in range(4):
                key = jnp.where(lane // 32 == i, codes[kk * 4 + i, z_to], key)
            keys[:, kk * TILE : (kk + 1) * TILE] = key

        def sum_owner(d, _, k=k):
            key = keys[pl.ds(d, 1), :]
            pick = jnp.where(row == key, 1.0, 0.0).astype(BF16)
            parts = got[k, :, pl.ds(d * SLOT, SLOT)].reshape(CLUSTER * SLOT * ROWS, TILE)
            sums[k, d] = jnp.dot(pick, parts, preferred_element_type=F32)
            return 0

        lax.fori_loop(0, YN, sum_owner, 0)

        for s in range(4):
            part = sums[k, (y + 4 - s) % 8]
            if s > 0:
                right_copy(k, s - 1).wait_recv()
                part += from_left[k, s - 1].astype(F32)
            to_right[k, s] = part.astype(BF16)
            right_copy(k, s).start()
            if s < 3:
                part = sums[k, (y + 5 + s) % 8]
                if s > 0:
                    left_copy(k, s - 1).wait_recv()
                    part += from_right[k, s - 1].astype(F32)
                to_left[k, s] = part.astype(BF16)
                left_copy(k, s).start()
        total = sums[k, y]
        left_copy(k, 2).wait_recv()
        total += from_right[k, 2].astype(F32)
        right_copy(k, 3).wait_recv()
        total += from_left[k, 3].astype(F32)
        if k < ZH - 1:
            to_z[k] = total.astype(BF16)
            z_copy(k).start()

    for k in range(ZH - 1):
        z_copy(k).wait_recv()
        total += from_z[k].astype(F32)
    mine = pl.ds(pl.multiple_of(group * ROWS, ROWS), ROWS)
    total += back_ref[:, mine, :].astype(F32).reshape(PIECE, TILE)
    out_ref[:, mine, :] = total.astype(BF16).reshape(OWNED, ROWS, TILE)

    def out_copy(n, way):
        g = (group + way * n + SLICES) % SLICES
        at = group if way == 1 else g
        there = out_ref.at[:, pl.ds(pl.multiple_of(at * ROWS, ROWS), ROWS), :]
        return pltpu.make_async_remote_copy(
            src_ref=there, dst_ref=there,
            send_sem=out_send.at[n], recv_sem=out_recv.at[n],
            device_id=device(z_hi, y, core, g), device_id_type=MESH,
        )

    def each_slice(do):
        def step(n, _):
            do(n)
            return 0

        lax.fori_loop(1, SLICES, step, 0)

    each_slice(lambda n: out_copy(n, 1).start())
    each_slice(lambda n: out_copy(n, -1).wait_recv())

    each_peer(lambda n: code_copy(n, 1).wait_send())
    for k in range(ZH):
        each_peer(lambda n, k=k: made_copy(k, n, 1).wait_send())
        for s in range(4):
            right_copy(k, s).wait_send()
        for s in range(3):
            left_copy(k, s).wait_send()
        if k < ZH - 1:
            z_copy(k).wait_send()
    each_slice(lambda n: out_copy(n, 1).wait_send())


def on_device(
    activations, grad_out, kept_rows, kept_cols, kept_count, owner_tiles, apply_mask, feedback_in
):
    vmem = pl.BlockSpec(memory_space=pltpu.VMEM)
    smem = pl.BlockSpec(memory_space=pltpu.SMEM)
    table, code = pl.pallas_call(
        prep_kernel,
        out_shape=(
            jax.ShapeDtypeStruct((2, TILE), jnp.int32),
            jax.ShapeDtypeStruct((CORES, ZH, YN, TILE), F32),
        ),
        in_specs=[smem, vmem, vmem, vmem],
        out_specs=(vmem, vmem),
    )(kept_count, kept_rows, kept_cols, owner_tiles.reshape(-1, TILE))

    dma = pltpu.SemaphoreType.DMA
    summed = pl.pallas_call(
        main_kernel,
        out_shape=jax.ShapeDtypeStruct(feedback_in.shape, BF16),
        in_specs=[smem, vmem, vmem, vmem, vmem],
        out_specs=vmem,
        scratch_shapes=[
            pltpu.VMEM((activations.shape[1] // TILE, TILE, TILE), BF16),
            pltpu.VMEM((grad_out.shape[1] // TILE, TILE, TILE), BF16),
            pltpu.VMEM((ZH, CORES, SLICES, PER_CHUNK, ROWS, TILE), BF16),
            pltpu.VMEM((ZH, CLUSTER, PER_CHUNK, ROWS, TILE), BF16),
            pltpu.VMEM((CLUSTER, ZH, YN, TILE), F32),
            pltpu.VMEM((YN, CLUSTER * SLOT * ROWS), F32),
            pltpu.VMEM((ZH, YN, PIECE, TILE), F32),
            pltpu.VMEM((ZH, 4, PIECE, TILE), BF16),
            pltpu.VMEM((ZH, 4, PIECE, TILE), BF16),
            pltpu.VMEM((ZH, 3, PIECE, TILE), BF16),
            pltpu.VMEM((ZH, 3, PIECE, TILE), BF16),
            pltpu.VMEM((ZH - 1, PIECE, TILE), BF16),
            pltpu.VMEM((ZH - 1, PIECE, TILE), BF16),
            dma((CLUSTER,)), dma((CLUSTER,)),
            dma((ZH, CLUSTER)), dma((ZH, CLUSTER)),
            dma((ZH, 4)), dma((ZH, 4)),
            dma((ZH, 3)), dma((ZH, 3)),
            dma((ZH - 1,)), dma((ZH - 1,)),
            dma((SLICES,)), dma((SLICES,)),
        ],
        compiler_params=pltpu.CompilerParams(
            collective_id=0, has_side_effects=True, vmem_limit_bytes=56 * 2**20
        ),
    )(table, code, activations, grad_out, feedback_in)
    applied = (apply_mask == 1)[:, None, None]
    zero = jnp.zeros((), BF16)
    return (jnp.where(applied, summed, zero), jnp.where(applied, zero, summed))


def solution(mesh):
    return jax.shard_map(
        on_device,
        mesh=mesh,
        in_specs=(
            P(("blk", "group"), None),
            P(("blk", "group"), None),
            P(("blk", "group"), None),
            P(("blk", "group"), None),
            P(("blk", "group")),
            P(),
            P("blk"),
            P("blk", None, None),
        ),
        out_specs=(P("blk", None, None), P("blk", None, None)),
        check_vma=False,
    )
```

```python
import functools

import jax
import jax.numpy as jnp
from jax import lax
from jax.experimental import pallas as pl
from jax.experimental.pallas import tpu as pltpu
from jax.sharding import PartitionSpec as P

ZH, YN, CORES, XN, ZL = 4, 8, 2, 4, 2
SLICES = XN * ZL
CLUSTER = SLICES * CORES
SLOT = 2
TILE = 128
ROWS = TILE // SLICES
OWNED = 20
PIECE = OWNED * ROWS
PER_CHUNK = YN * SLOT
PARTS = 16
AHEAD = 6
MESH = pl.DeviceIdType.MESH
F32 = jnp.float32
BF16 = jnp.bfloat16


def prep_kernel(count_ref, rows_ref, cols_ref, tiles_ref, table_ref, code_ref):
    n = TILE
    sub = lax.broadcasted_iota(jnp.int32, (n, n), 0).astype(F32)
    lane = lax.broadcasted_iota(jnp.int32, (n, n), 1).astype(F32)
    count = count_ref[0].astype(F32)
    row_of = jnp.broadcast_to(rows_ref[...].astype(F32), (n, n)).T
    col_of = jnp.broadcast_to(cols_ref[...].astype(F32), (n, n)).T
    tile_of = row_of * 64.0 + col_of
    found = jnp.zeros((n, n), F32)
    for k in range(tiles_ref.shape[0]):
        known = tiles_ref[k : k + 1, :].astype(F32)
        found += jnp.where(tile_of == known, lane + 128.0 * k, 0.0)
    position = jnp.broadcast_to(jnp.sum(found, axis=1, keepdims=True), (n, n))
    owner = jnp.floor((position + 0.5) * (1.0 / OWNED))
    label = position - OWNED * owner
    same = (owner.T == owner) & (lane < sub) & (lane < count)
    rank = jnp.sum(jnp.where(same, 1.0, 0.0), axis=1, keepdims=True)
    z_hi = jnp.floor((owner + 0.5) * (1.0 / 16.0))
    in_plane = owner - 16.0 * z_hi
    y = jnp.floor((in_plane + 0.5) * 0.5)
    core = in_plane - 2.0 * y
    slot = ((z_hi * 2.0 + core) * 8.0 + y) * 2.0 + rank
    chosen = (slot == lane) & (sub < count)
    slot_row = jnp.sum(jnp.where(chosen, row_of, 0.0), axis=0, keepdims=True)
    slot_col = jnp.sum(jnp.where(chosen, col_of, 0.0), axis=0, keepdims=True)
    slot_label = jnp.sum(jnp.where(chosen, label + 1.0, 0.0), axis=0, keepdims=True) - 1.0
    table_ref[0:1, :] = slot_row.astype(jnp.int32)
    table_ref[1:2, :] = slot_col.astype(jnp.int32)
    m = CORES * YN
    at = lax.broadcasted_iota(jnp.int32, (m, n), 0)
    s = lax.broadcasted_iota(jnp.int32, (m, n), 1)
    mine = (s // 16) % 2 * 8 + (s // 2) % 8 == at
    spread = jnp.where(mine, jnp.broadcast_to(slot_label, (m, n)), 0.0).astype(BF16)
    s2 = lax.broadcasted_iota(jnp.int32, (n, n), 0)
    l2 = lax.broadcasted_iota(jnp.int32, (n, n), 1)
    pick = jnp.where((s2 // 32 == l2 // 32) & (s2 % 2 == l2 // 16 % 2), 1.0, 0.0).astype(BF16)
    coded = jnp.dot(spread, pick, preferred_element_type=F32) * 16.0
    coded += (lax.broadcasted_iota(jnp.int32, (m, n), 1) % 16).astype(F32)
    code_ref[...] = coded.reshape(CORES, YN, n)


def main_kernel(
    table_ref, code_ref, act_ref, grad_ref, back_ref, out_ref,
    act_t, grad_t, other, made, got, codes, keys, own,
    to_right, from_left, to_left, from_right, to_z, from_z,
    code_send, code_recv, swap_send, swap_recv, made_send, made_recv,
    right_send, right_recv, left_send, left_recv, z_send, z_recv, out_send, out_recv,
):
    blk = lax.axis_index("blk")
    group = lax.axis_index("group")
    z_hi, y, core = blk // 16, (blk // 2) % 8, blk % 2
    x, z_lo = group // 2, group % 2
    me = group * 2 + core

    def device(z_hi_at, y_at, core_at, group_at):
        return ((z_hi_at * 8 + y_at) * 2 + core_at, group_at)

    def member(n, way):
        return ((x + way * (n // 2) + XN) % XN) * 2 + (z_lo + n % 2) % 2

    def remote(src, dst, send, recv, to):
        return pltpu.make_async_remote_copy(
            src_ref=src, dst_ref=dst, send_sem=send, recv_sem=recv,
            device_id=to, device_id_type=MESH,
        )

    def each(stop, do):
        def step(n, _):
            do(n)
            return 0

        lax.fori_loop(1, stop, step, 0)

    right = device(z_hi, (y + 1) % 8, core, group)
    left = device(z_hi, (y + 7) % 8, core, group)
    sibling = device(z_hi, y, 1 - core, group)

    barrier = pltpu.get_barrier_semaphore()

    def greet(to):
        pl.semaphore_signal(barrier, inc=1, device_id=to, device_id_type=MESH)

    each(CLUSTER, lambda n: greet(device(z_hi, y, (core + n % 2) % 2, member(n // 2, 1))))
    greet(right)
    greet(left)
    each(ZH, lambda k: greet(device((z_hi + k) % 4, y, core, group)))

    def turn(r, _):
        act_t[r] = act_ref[:, pl.ds(pl.multiple_of(r * TILE, TILE), TILE)].T
        return 0

    lax.fori_loop(0, act_ref.shape[1] // TILE, turn, 0, unroll=4)

    def part(r, _):
        grad_t[r] = grad_ref[:, pl.ds(pl.multiple_of(r * TILE, TILE), TILE)]
        return 0

    lax.fori_loop(0, grad_ref.shape[1] // TILE, part, 0, unroll=4)

    def order(m):
        return m // 8 * 2 + m % 2, m // 2 % 4

    def plane(k):
        return (z_hi + 1 + k) % 4

    def pair(p):
        return (y + 4 - p) % 8, (y + 5 + p) % 8

    def make(m):
        k, p = order(m)

        def tile(c, o, j):
            e = (plane(k) * 2 + c) * PER_CHUNK + pair(p)[o] * SLOT + j
            a, b = act_t[table_ref[0, e]], grad_t[table_ref[1, e]]
            product = jnp.dot(a, b, preferred_element_type=F32).astype(BF16)
            return product.reshape(SLICES, ROWS, TILE)

        for o in range(2):
            for j in range(SLOT):
                other[m, :, o * SLOT + j] = tile(1 - core, o, j)
        for o in range(2):
            for j in range(SLOT):
                made[m, :, core, o * SLOT + j] = tile(core, o, j)

    def code_copy(n, way):
        g, c = member(n // 2, way), (core + n % 2) % 2
        return remote(
            code_ref.at[c], codes.at[me if way == 1 else g * 2 + c],
            code_send.at[n], code_recv.at[n], device(z_hi, y, c, g),
        )

    def swap(m, way):
        there = made.at[m, :, core if way == 1 else 1 - core]
        return remote(other.at[m], there, swap_send.at[m], swap_recv.at[m], sibling)

    def made_copy(m, n, way):
        g = member(n, way)
        return remote(
            made.at[m, g], got.at[m, group if way == 1 else g],
            made_send.at[m, n], made_recv.at[m, n], device(z_hi, y, core, g),
        )

    def right_copy(k, s):
        return remote(
            to_right.at[k, s], from_left.at[k, s], right_send.at[k, s], right_recv.at[k, s], right
        )

    def left_copy(k, s):
        return remote(
            to_left.at[k, s], from_right.at[k, s], left_send.at[k, s], left_recv.at[k, s], left
        )

    def z_copy(k):
        to = device(plane(k), y, core, group)
        return remote(to_z.at[k], from_z.at[k], z_send.at[k], z_recv.at[k], to)

    def out_copy(n, way):
        g = member(n, way)
        at = group if way == 1 else g
        there = out_ref.at[:, pl.ds(pl.multiple_of(at * ROWS, ROWS), ROWS), :]
        return remote(there, there, out_send.at[n], out_recv.at[n], device(z_hi, y, core, g))

    def send(m):
        swap(m, -1).wait_recv()
        each(SLICES, lambda n: made_copy(m, n, 1).start())

    lane = lax.broadcasted_iota(jnp.int32, (YN, TILE), 1)
    row = lax.broadcasted_iota(jnp.int32, (PIECE, CLUSTER * SLOT * ROWS), 0).astype(F32)

    def line_up(k):
        for kk in range(4):
            key = jnp.zeros((YN, TILE), F32)
            for i in range(4):
                turned = pltpu.roll(codes[kk * 4 + i], (i + 4 - plane(k)) % 4 * 32, 1)
                key = jnp.where(lane // 32 == i, turned, key)
            keys[k, :, kk * TILE : (kk + 1) * TILE] = key

    def owner_sum(m, o):
        k, p = order(m)
        pick = jnp.where(row == keys[k, pl.ds(pair(p)[o], 1), :], 1.0, 0.0).astype(BF16)
        parts = got[m, :, :, o * SLOT : (o + 1) * SLOT].reshape(CLUSTER * SLOT * ROWS, TILE)
        return jnp.dot(pick, parts, preferred_element_type=F32)

    def finish(k):
        left_copy(k, 2).wait_recv()
        right_copy(k, 3).wait_recv()
        total = own[k] + from_right[k, 2].astype(F32) + from_left[k, 3].astype(F32)
        if k < ZH - 1:
            to_z[k] = total.astype(BF16)
            z_copy(k).start()
        return total

    make(0)
    pl.semaphore_wait(barrier, CLUSTER - 1 + 2 + ZH - 1)
    swap(0, 1).start()
    each(CLUSTER, lambda n: code_copy(n, 1).start())
    codes[me] = code_ref[core]
    for m in range(1, AHEAD + 1):
        make(m)
        swap(m, 1).start()
        send(m - 1)
    each(CLUSTER, lambda n: code_copy(n, -1).wait_recv())
    for k in range(ZH):
        line_up(k)

    total = None
    for m in range(PARTS):
        k, p = order(m)
        if m + AHEAD + 1 < PARTS:
            make(m + AHEAD + 1)
            swap(m + AHEAD + 1, 1).start()
        if m + AHEAD < PARTS:
            send(m + AHEAD)
        got[m, group] = made[m, group]
        each(SLICES, lambda n, m=m: made_copy(m, n, -1).wait_recv())
        rightward = owner_sum(m, 0)
        if p > 0:
            right_copy(k, p - 1).wait_recv()
            rightward += from_left[k, p - 1].astype(F32)
        to_right[k, p] = rightward.astype(BF16)
        right_copy(k, p).start()
        leftward = owner_sum(m, 1)
        if p < 3:
            if p > 0:
                left_copy(k, p - 1).wait_recv()
                leftward += from_right[k, p - 1].astype(F32)
            to_left[k, p] = leftward.astype(BF16)
            left_copy(k, p).start()
        else:
            own[k] = leftward
        if m > 0 and order(m - 1)[1] == 3:
            finish(order(m - 1)[0])
    total = finish(ZH - 1)

    for k in range(ZH - 1):
        z_copy(k).wait_recv()
        total += from_z[k].astype(F32)
    mine = pl.ds(pl.multiple_of(group * ROWS, ROWS), ROWS)
    total += back_ref[:, mine, :].astype(F32).reshape(PIECE, TILE)
    out_ref[:, mine, :] = total.astype(BF16).reshape(OWNED, ROWS, TILE)
    each(SLICES, lambda n: out_copy(n, 1).start())
    each(SLICES, lambda n: out_copy(n, -1).wait_recv())

    each(CLUSTER, lambda n: code_copy(n, 1).wait_send())
    for m in range(PARTS):
        swap(m, 1).wait_send()
        each(SLICES, lambda n, m=m: made_copy(m, n, 1).wait_send())
    for k in range(ZH):
        for s in range(4):
            right_copy(k, s).wait_send()
        for s in range(3):
            left_copy(k, s).wait_send()
        if k < ZH - 1:
            z_copy(k).wait_send()
    each(SLICES, lambda n: out_copy(n, 1).wait_send())


def split_kernel(mask_ref, summed_ref, update_ref, feedback_ref):
    rows = summed_ref.shape[0]
    for t in range(rows):
        applied = mask_ref[pl.program_id(0) * rows + t] == 1
        summed = summed_ref[t].astype(F32)
        update_ref[t] = jnp.where(applied, summed, 0.0).astype(BF16)
        feedback_ref[t] = jnp.where(applied, 0.0, summed).astype(BF16)


def on_device(
    activations, grad_out, kept_rows, kept_cols, kept_count, owner_tiles, apply_mask, feedback_in
):
    vmem = pl.BlockSpec(memory_space=pltpu.VMEM)
    smem = pl.BlockSpec(memory_space=pltpu.SMEM)
    table, code = pl.pallas_call(
        prep_kernel,
        out_shape=(
            jax.ShapeDtypeStruct((2, TILE), jnp.int32),
            jax.ShapeDtypeStruct((CORES, YN, TILE), F32),
        ),
        in_specs=[smem, vmem, vmem, vmem],
        out_specs=(vmem, vmem),
    )(kept_count, kept_rows, kept_cols, owner_tiles.reshape(-1, TILE))

    dma = pltpu.SemaphoreType.DMA
    summed = pl.pallas_call(
        main_kernel,
        out_shape=jax.ShapeDtypeStruct(feedback_in.shape, BF16),
        in_specs=[smem, vmem, vmem, vmem, vmem],
        out_specs=vmem,
        scratch_shapes=[
            pltpu.VMEM((activations.shape[1] // TILE, TILE, TILE), BF16),
            pltpu.VMEM((grad_out.shape[1] // TILE, TILE, TILE), BF16),
            pltpu.VMEM((PARTS, SLICES, 2 * SLOT, ROWS, TILE), BF16),
            pltpu.VMEM((PARTS, SLICES, CORES, 2 * SLOT, ROWS, TILE), BF16),
            pltpu.VMEM((PARTS, SLICES, CORES, 2 * SLOT, ROWS, TILE), BF16),
            pltpu.VMEM((CLUSTER, YN, TILE), F32),
            pltpu.VMEM((ZH, YN, CLUSTER * SLOT * ROWS), F32),
            pltpu.VMEM((ZH, PIECE, TILE), F32),
            pltpu.VMEM((ZH, 4, PIECE, TILE), BF16),
            pltpu.VMEM((ZH, 4, PIECE, TILE), BF16),
            pltpu.VMEM((ZH, 3, PIECE, TILE), BF16),
            pltpu.VMEM((ZH, 3, PIECE, TILE), BF16),
            pltpu.VMEM((ZH - 1, PIECE, TILE), BF16),
            pltpu.VMEM((ZH - 1, PIECE, TILE), BF16),
            dma((CLUSTER,)), dma((CLUSTER,)),
            dma((PARTS,)), dma((PARTS,)),
            dma((PARTS, SLICES)), dma((PARTS, SLICES)),
            dma((ZH, 4)), dma((ZH, 4)),
            dma((ZH, 3)), dma((ZH, 3)),
            dma((ZH - 1,)), dma((ZH - 1,)),
            dma((SLICES,)), dma((SLICES,)),
        ],
        compiler_params=pltpu.CompilerParams(
            collective_id=0, has_side_effects=True, vmem_limit_bytes=56 * 2**20
        ),
    )(table, code, activations, grad_out, feedback_in)
    some = pl.BlockSpec((5, TILE, TILE), lambda i: (i, 0, 0))
    return tuple(
        pl.pallas_call(
            split_kernel,
            grid=(feedback_in.shape[0] // 5,),
            out_shape=(jax.ShapeDtypeStruct(feedback_in.shape, BF16),) * 2,
            in_specs=[smem, some],
            out_specs=(some, some),
        )(apply_mask, summed)
    )


def solution(mesh):
    return jax.shard_map(
        on_device,
        mesh=mesh,
        in_specs=(
            P(("blk", "group"), None),
            P(("blk", "group"), None),
            P(("blk", "group"), None),
            P(("blk", "group"), None),
            P(("blk", "group")),
            P(),
            P("blk"),
            P("blk", None, None),
        ),
        out_specs=(P("blk", None, None), P("blk", None, None)),
        check_vma=False,
    )
```

```python
import functools

import jax
import jax.numpy as jnp
from jax import lax
from jax.experimental import pallas as pl
from jax.experimental.pallas import tpu as pltpu
from jax.sharding import PartitionSpec as P

ZH, YN, CORES, XN, ZL = 4, 8, 2, 4, 2
SLICES = XN * ZL
CLUSTER = SLICES * CORES
SLOT = 2
TILE = 128
ROWS = TILE // SLICES
OWNED = 20
PIECE = OWNED * ROWS
PER_CHUNK = YN * SLOT
PARTS = 16
AHEAD = 9
ORDER = (
    (0, 0), (0, 1), (1, 0), (0, 2), (1, 1), (0, 3), (1, 2), (2, 0),
    (1, 3), (2, 1), (3, 0), (2, 2), (3, 1), (2, 3), (3, 2), (3, 3),
)
SPLIT = 10
MESH = pl.DeviceIdType.MESH
F32 = jnp.float32
BF16 = jnp.bfloat16


def index_work(count_ref, rows_ref, cols_ref, tiles_ref, table_ref, code_ref):
    n = TILE
    sub = lax.broadcasted_iota(jnp.int32, (n, n), 0).astype(F32)
    lane = lax.broadcasted_iota(jnp.int32, (n, n), 1).astype(F32)
    count = count_ref[0].astype(F32)
    row_of = jnp.broadcast_to(rows_ref[...].astype(F32), (n, n)).T
    col_of = jnp.broadcast_to(cols_ref[...].astype(F32), (n, n)).T
    tile_of = row_of * 64.0 + col_of
    found = jnp.zeros((n, n), F32)
    for k in range(tiles_ref.shape[0]):
        known = tiles_ref[k : k + 1, :].astype(F32)
        found += jnp.where(tile_of == known, lane + 128.0 * k, 0.0)
    position = jnp.broadcast_to(jnp.sum(found, axis=1, keepdims=True), (n, n))
    owner = jnp.floor((position + 0.5) * (1.0 / OWNED))
    label = position - OWNED * owner
    same = (owner.T == owner) & (lane < sub) & (lane < count)
    rank = jnp.sum(jnp.where(same, 1.0, 0.0), axis=1, keepdims=True)
    z_hi = jnp.floor((owner + 0.5) * (1.0 / 16.0))
    in_plane = owner - 16.0 * z_hi
    y = jnp.floor((in_plane + 0.5) * 0.5)
    core = in_plane - 2.0 * y
    slot = ((z_hi * 2.0 + core) * 8.0 + y) * 2.0 + rank
    chosen = (slot == lane) & (sub < count)
    slot_row = jnp.sum(jnp.where(chosen, row_of, 0.0), axis=0, keepdims=True)
    slot_col = jnp.sum(jnp.where(chosen, col_of, 0.0), axis=0, keepdims=True)
    slot_label = jnp.sum(jnp.where(chosen, label + 1.0, 0.0), axis=0, keepdims=True) - 1.0
    table_ref[0:1, :] = slot_row.astype(jnp.int32)
    table_ref[1:2, :] = slot_col.astype(jnp.int32)
    m = CORES * YN
    at = lax.broadcasted_iota(jnp.int32, (m, n), 0)
    s = lax.broadcasted_iota(jnp.int32, (m, n), 1)
    mine = (s // 16) % 2 * 8 + (s // 2) % 8 == at
    spread = jnp.where(mine, jnp.broadcast_to(slot_label, (m, n)), 0.0).astype(BF16)
    s2 = lax.broadcasted_iota(jnp.int32, (n, n), 0)
    l2 = lax.broadcasted_iota(jnp.int32, (n, n), 1)
    pick = jnp.where((s2 // 32 == l2 // 32) & (s2 % 2 == l2 // 16 % 2), 1.0, 0.0).astype(BF16)
    coded = jnp.dot(spread, pick, preferred_element_type=F32) * 16.0
    coded += (lax.broadcasted_iota(jnp.int32, (m, n), 1) % 16).astype(F32)
    code_ref[...] = coded.reshape(CORES, YN, n)


def main_kernel(
    count_ref, rows_ref, cols_ref, tiles_ref, act_hbm, grad_hbm, back_hbm, out_ref,
    act_ref, grad_ref, back_ref, table_made, table_ref, code_ref,
    act_t, grad_t, other, made, got, codes, keys, own,
    to_right, from_left, to_left, from_right, to_z, from_z,
    load, code_send, code_recv, swap_send, swap_recv, made_send, made_recv,
    right_send, right_recv, left_send, left_recv, z_send, z_recv, out_send, out_recv,
):
    blk = lax.axis_index("blk")
    group = lax.axis_index("group")
    z_hi, y, core = blk // 16, (blk // 2) % 8, blk % 2
    x, z_lo = group // 2, group % 2
    me = group * 2 + core

    def device(z_hi_at, y_at, core_at, group_at):
        return ((z_hi_at * 8 + y_at) * 2 + core_at, group_at)

    def member(n, way):
        return ((x + way * (n // 2) + XN) % XN) * 2 + (z_lo + n % 2) % 2

    def remote(src, dst, send, recv, to):
        return pltpu.make_async_remote_copy(
            src_ref=src, dst_ref=dst, send_sem=send, recv_sem=recv,
            device_id=to, device_id_type=MESH,
        )

    def each(stop, do):
        def step(n, _):
            do(n)
            return 0

        lax.fori_loop(1, stop, step, 0)

    right = device(z_hi, (y + 1) % 8, core, group)
    left = device(z_hi, (y + 7) % 8, core, group)
    sibling = device(z_hi, y, 1 - core, group)

    loads = [
        pltpu.make_async_copy(there, here, load.at[i])
        for i, (there, here) in enumerate(
            [(act_hbm, act_ref), (grad_hbm, grad_ref), (back_hbm, back_ref)]
        )
    ]
    for copy in loads:
        copy.start()

    barrier = pltpu.get_barrier_semaphore()

    def greet(to):
        pl.semaphore_signal(barrier, inc=1, device_id=to, device_id_type=MESH)

    greet(sibling)
    each(SLICES, lambda n: greet(device(z_hi, y, core, member(n, 1))))
    greet(right)
    greet(left)
    each(ZH, lambda k: greet(device((z_hi + k) % 4, y, core, group)))

    index_work(count_ref, rows_ref, cols_ref, tiles_ref, table_made, code_ref)
    table = pltpu.make_async_copy(table_made, table_ref, load.at[3])
    table.start()
    loads[0].wait()

    def turn(r, _):
        act_t[r] = act_ref[:, pl.ds(pl.multiple_of(r * TILE, TILE), TILE)].T
        return 0

    lax.fori_loop(0, act_ref.shape[1] // TILE, turn, 0, unroll=4)

    loads[1].wait()

    def part(r, _):
        grad_t[r] = grad_ref[:, pl.ds(pl.multiple_of(r * TILE, TILE), TILE)]
        return 0

    lax.fori_loop(0, grad_ref.shape[1] // TILE, part, 0, unroll=4)

    def plane(k):
        return (z_hi + 1 + k) % 4

    def pair(p):
        return (y + 4 - p) % 8, (y + 5 + p) % 8

    def make(m):
        k, p = ORDER[m]

        def tile(core_to, o, j):
            e = (plane(k) * 2 + core_to) * PER_CHUNK + pair(p)[o] * SLOT + j
            r = jnp.clip(table_ref[0, e], 0, act_t.shape[0] - 1)
            c = jnp.clip(table_ref[1, e], 0, grad_t.shape[0] - 1)
            a, b = act_t[r], grad_t[c]
            product = jnp.dot(a, b, preferred_element_type=F32).astype(BF16)
            return product.reshape(SLICES, ROWS, TILE)

        for o in range(2):
            for j in range(SLOT):
                other[m, :, o * SLOT + j] = tile(1 - core, o, j)
        for o in range(2):
            for j in range(SLOT):
                made[m, :, core, o * SLOT + j] = tile(core, o, j)

    def code_swap(way):
        there = codes.at[group, core if way == 1 else 1 - core]
        return remote(code_ref.at[1 - core], there, code_send.at[0], code_recv.at[0], sibling)

    def code_copy(n):
        mine = codes.at[group]
        to = device(z_hi, y, core, member(n, 1))
        return remote(mine, mine, code_send.at[1], code_recv.at[1], to)

    def swap(m, way):
        there = made.at[m, :, core if way == 1 else 1 - core]
        return remote(other.at[m], there, swap_send.at[0], swap_recv.at[m], sibling)

    def made_copy(m, n):
        to = device(z_hi, y, core, member(n, 1))
        return remote(made.at[m, member(n, 1)], got.at[m, group], made_send.at[0], made_recv.at[m], to)

    def all_of(ref, semaphore):
        pltpu.make_async_copy(ref, ref, semaphore).wait()

    def right_copy(k, s):
        return remote(
            to_right.at[k, s], from_left.at[k, s], right_send.at[0], right_recv.at[k, s], right
        )

    def left_copy(k, s):
        return remote(
            to_left.at[k, s], from_right.at[k, s], left_send.at[0], left_recv.at[k, s], left
        )

    def z_copy(k):
        to = device(plane(k), y, core, group)
        return remote(to_z.at[k], from_z.at[k], z_send.at[0], z_recv.at[k], to)

    def out_copy(n):
        there = out_ref.at[group]
        to = device(z_hi, y, core, member(n, 1))
        return remote(there, there, out_send.at[0], out_recv.at[0], to)

    def send(m):
        swap(m, -1).wait_recv()
        each(SLICES, lambda n: made_copy(m, n).start())

    lane = lax.broadcasted_iota(jnp.int32, (YN, TILE), 1)
    row = lax.broadcasted_iota(jnp.int32, (PIECE, CLUSTER * SLOT * ROWS), 0).astype(F32)

    def line_up(k):
        for kk in range(4):
            key = jnp.zeros((YN, TILE), F32)
            for i in range(4):
                turned = pltpu.roll(codes[kk * 2 + i // 2, i % 2], (i + 4 - plane(k)) % 4 * 32, 1)
                key = jnp.where(lane // 32 == i, turned, key)
            keys[k, :, kk * TILE : (kk + 1) * TILE] = key

    def owner_sum(m, o):
        k, p = ORDER[m]
        pick = jnp.where(row == keys[k, pl.ds(pair(p)[o], 1), :], 1.0, 0.0).astype(BF16)
        parts = got[m, :, :, o * SLOT : (o + 1) * SLOT].reshape(CLUSTER * SLOT * ROWS, TILE)
        return jnp.dot(pick, parts, preferred_element_type=F32)

    def finish(k):
        left_copy(k, 2).wait_recv()
        right_copy(k, 3).wait_recv()
        total = own[k] + from_right[k, 2].astype(F32) + from_left[k, 3].astype(F32)
        if k < ZH - 1:
            to_z[k] = total.astype(BF16)
            z_copy(k).start()
        return total

    table.wait()
    make(0)
    pl.semaphore_wait(barrier, 1 + SLICES - 1 + 2 + ZH - 1)
    swap(0, 1).start()
    code_swap(1).start()
    codes[group, core] = code_ref[core]
    for m in range(1, AHEAD + 1):
        make(m)
        swap(m, 1).start()
        send(m - 1)
        if m == 1:
            code_swap(-1).wait_recv()
            each(SLICES, lambda n: code_copy(n).start())
    all_of(codes.at[1:], code_recv.at[1])
    for k in range(ZH):
        line_up(k)

    total = None
    for m in range(PARTS):
        k, p = ORDER[m]
        if m + AHEAD + 1 < PARTS:
            make(m + AHEAD + 1)
            swap(m + AHEAD + 1, 1).start()
        if m + AHEAD < PARTS:
            send(m + AHEAD)
        got[m, group] = made[m, group]
        all_of(got.at[m, 1:], made_recv.at[m])
        rightward = owner_sum(m, 0)
        if p > 0:
            right_copy(k, p - 1).wait_recv()
            rightward += from_left[k, p - 1].astype(F32)
        to_right[k, p] = rightward.astype(BF16)
        right_copy(k, p).start()
        leftward = owner_sum(m, 1)
        if p < 3:
            if p > 0:
                left_copy(k, p - 1).wait_recv()
                leftward += from_right[k, p - 1].astype(F32)
            to_left[k, p] = leftward.astype(BF16)
            left_copy(k, p).start()
        else:
            own[k] = leftward
        if m > 0 and ORDER[m - 1][1] == 3:
            finish(ORDER[m - 1][0])
    total = finish(ZH - 1)

    for k in range(ZH - 1):
        z_copy(k).wait_recv()
        total += from_z[k].astype(F32)
    loads[2].wait()
    mine = pl.ds(pl.multiple_of(group * ROWS, ROWS), ROWS)
    total += back_ref[:, mine, :].astype(F32).reshape(PIECE, TILE)
    out_ref[group] = total.astype(BF16).reshape(OWNED, ROWS, TILE)
    each(SLICES, lambda n: out_copy(n).start())
    all_of(out_ref.at[1:], out_recv.at[0])

    code_swap(1).wait_send()
    all_of(codes.at[1:], code_send.at[1])
    all_of(other, swap_send.at[0])
    all_of(made.at[: PARTS * (SLICES - 1) // SLICES], made_send.at[0])
    all_of(to_right, right_send.at[0])
    all_of(to_left, left_send.at[0])
    all_of(to_z, z_send.at[0])
    all_of(out_ref.at[1:], out_send.at[0])


def split_kernel(mask_ref, summed_ref, update_ref, feedback_ref):
    tiles = update_ref.shape[0]
    for t in range(tiles):
        applied = mask_ref[pl.program_id(0) * tiles + t] == 1
        for g in range(SLICES):
            summed = summed_ref[g, t].astype(F32)
            at = slice(g * ROWS, (g + 1) * ROWS)
            update_ref[t, at] = jnp.where(applied, summed, 0.0).astype(BF16)
            feedback_ref[t, at] = jnp.where(applied, 0.0, summed).astype(BF16)


def on_device(
    activations, grad_out, kept_rows, kept_cols, kept_count, owner_tiles, apply_mask, feedback_in
):
    vmem = pl.BlockSpec(memory_space=pltpu.VMEM)
    smem = pl.BlockSpec(memory_space=pltpu.SMEM)
    anywhere = pl.BlockSpec(memory_space=pl.ANY)
    dma = pltpu.SemaphoreType.DMA
    summed = pl.pallas_call(
        main_kernel,
        out_shape=jax.ShapeDtypeStruct((SLICES, OWNED, ROWS, TILE), BF16),
        in_specs=[smem, vmem, vmem, vmem, anywhere, anywhere, anywhere],
        out_specs=vmem,
        scratch_shapes=[
            pltpu.VMEM(activations.shape, BF16),
            pltpu.VMEM(grad_out.shape, BF16),
            pltpu.VMEM(feedback_in.shape, BF16),
            pltpu.VMEM((2, TILE), jnp.int32),
            pltpu.SMEM((2, TILE), jnp.int32),
            pltpu.VMEM((CORES, YN, TILE), F32),
            pltpu.VMEM((activations.shape[1] // TILE, TILE, TILE), BF16),
            pltpu.VMEM((grad_out.shape[1] // TILE, TILE, TILE), BF16),
            pltpu.VMEM((PARTS, SLICES, 2 * SLOT, ROWS, TILE), BF16),
            pltpu.VMEM((PARTS, SLICES, CORES, 2 * SLOT, ROWS, TILE), BF16),
            pltpu.VMEM((PARTS, SLICES, CORES, 2 * SLOT, ROWS, TILE), BF16),
            pltpu.VMEM((SLICES, CORES, YN, TILE), F32),
            pltpu.VMEM((ZH, YN, CLUSTER * SLOT * ROWS), F32),
            pltpu.VMEM((ZH, PIECE, TILE), F32),
            pltpu.VMEM((ZH, 4, PIECE, TILE), BF16),
            pltpu.VMEM((ZH, 4, PIECE, TILE), BF16),
            pltpu.VMEM((ZH, 3, PIECE, TILE), BF16),
            pltpu.VMEM((ZH, 3, PIECE, TILE), BF16),
            pltpu.VMEM((ZH - 1, PIECE, TILE), BF16),
            pltpu.VMEM((ZH - 1, PIECE, TILE), BF16),
            dma((4,)),
            dma((2,)), dma((2,)),
            dma((1,)), dma((PARTS,)),
            dma((1,)), dma((PARTS,)),
            dma((1,)), dma((ZH, 4)),
            dma((1,)), dma((ZH, 3)),
            dma((1,)), dma((ZH - 1,)),
            dma((1,)), dma((1,)),
        ],
        compiler_params=pltpu.CompilerParams(
            collective_id=0, has_side_effects=True, vmem_limit_bytes=56 * 2**20
        ),
    )(
        kept_count, kept_rows, kept_cols, owner_tiles.reshape(-1, TILE),
        activations, grad_out, feedback_in,
    )
    some = pl.BlockSpec((SPLIT, TILE, TILE), lambda i: (i, 0, 0))
    return tuple(
        pl.pallas_call(
            split_kernel,
            grid=(OWNED // SPLIT,),
            out_shape=(jax.ShapeDtypeStruct(feedback_in.shape, BF16),) * 2,
            in_specs=[smem, pl.BlockSpec((SLICES, SPLIT, ROWS, TILE), lambda i: (0, i, 0, 0))],
            out_specs=(some, some),
        )(apply_mask, summed)
    )


def solution(mesh):
    return jax.shard_map(
        on_device,
        mesh=mesh,
        in_specs=(
            P(("blk", "group"), None),
            P(("blk", "group"), None),
            P(("blk", "group"), None),
            P(("blk", "group"), None),
            P(("blk", "group")),
            P(),
            P("blk"),
            P("blk", None, None),
        ),
        out_specs=(P("blk", None, None), P("blk", None, None)),
        check_vma=False,
    )
```

```python
import functools

import jax
import jax.numpy as jnp
from jax import lax
from jax.experimental import pallas as pl
from jax.experimental.pallas import tpu as pltpu
from jax.sharding import PartitionSpec as P

ZH, YN, CORES, XN, ZL = 4, 8, 2, 4, 2
SLICES = XN * ZL
CLUSTER = SLICES * CORES
SLOT = 2
TILE = 128
ROWS = TILE // SLICES
OWNED = 20
PIECE = OWNED * ROWS
PER_CHUNK = YN * SLOT
PARTS = 16
AHEAD = 9
ORDER = (
    (0, 0), (1, 0), (2, 0), (0, 1), (1, 1), (2, 1), (0, 2), (1, 2),
    (3, 0), (2, 2), (0, 3), (3, 1), (2, 3), (1, 3), (3, 2), (3, 3),
)
FAR_FIRST = (4, 5, 2, 6, 3, 7, 1)
HALF = PIECE // 2
MESH = pl.DeviceIdType.MESH
F32 = jnp.float32
BF16 = jnp.bfloat16


def index_work(count_ref, rows_ref, cols_ref, tiles_ref, table_ref, code_ref):
    n = TILE
    sub = lax.broadcasted_iota(jnp.int32, (n, n), 0).astype(F32)
    lane = lax.broadcasted_iota(jnp.int32, (n, n), 1).astype(F32)
    count = count_ref[0].astype(F32)
    row_of = jnp.broadcast_to(rows_ref[...].astype(F32), (n, n)).T
    col_of = jnp.broadcast_to(cols_ref[...].astype(F32), (n, n)).T
    tile_of = row_of * 64.0 + col_of
    found = jnp.zeros((n, n), F32)
    for k in range(tiles_ref.shape[0]):
        known = tiles_ref[k : k + 1, :].astype(F32)
        found += jnp.where(tile_of == known, lane + 128.0 * k, 0.0)
    position = jnp.broadcast_to(jnp.sum(found, axis=1, keepdims=True), (n, n))
    owner = jnp.floor((position + 0.5) * (1.0 / OWNED))
    label = position - OWNED * owner
    same = (owner.T == owner) & (lane < sub) & (lane < count)
    rank = jnp.sum(jnp.where(same, 1.0, 0.0), axis=1, keepdims=True)
    z_hi = jnp.floor((owner + 0.5) * (1.0 / 16.0))
    in_plane = owner - 16.0 * z_hi
    y = jnp.floor((in_plane + 0.5) * 0.5)
    core = in_plane - 2.0 * y
    slot = ((z_hi * 2.0 + core) * 8.0 + y) * 2.0 + rank
    chosen = (slot == lane) & (sub < count)
    slot_row = jnp.sum(jnp.where(chosen, row_of, 0.0), axis=0, keepdims=True)
    slot_col = jnp.sum(jnp.where(chosen, col_of, 0.0), axis=0, keepdims=True)
    slot_label = jnp.sum(jnp.where(chosen, label + 1.0, 0.0), axis=0, keepdims=True) - 1.0
    table_ref[0:1, :] = slot_row.astype(jnp.int32)
    table_ref[1:2, :] = slot_col.astype(jnp.int32)
    m = CORES * YN
    at = lax.broadcasted_iota(jnp.int32, (m, n), 0)
    s = lax.broadcasted_iota(jnp.int32, (m, n), 1)
    mine = (s // 16) % 2 * 8 + (s // 2) % 8 == at
    spread = jnp.where(mine, jnp.broadcast_to(slot_label, (m, n)), 0.0).astype(BF16)
    s2 = lax.broadcasted_iota(jnp.int32, (n, n), 0)
    l2 = lax.broadcasted_iota(jnp.int32, (n, n), 1)
    pick = jnp.where((s2 // 32 == l2 // 32) & (s2 % 2 == l2 // 16 % 2), 1.0, 0.0).astype(BF16)
    coded = jnp.dot(spread, pick, preferred_element_type=F32) * 16.0
    coded += (lax.broadcasted_iota(jnp.int32, (m, n), 1) % 16).astype(F32)
    code_ref[...] = coded.reshape(CORES, YN, n)


def main_kernel(
    count_ref, rows_ref, cols_ref, tiles_ref, act_hbm, grad_hbm, back_hbm, out_ref,
    act_ref, grad_ref, back_ref, table_made, table_ref, code_ref,
    act_t, grad_t, other, made, got, codes, keys, own,
    to_right, from_left, to_left, from_right, to_z, from_z,
    load, code_send, code_recv, swap_send, swap_recv, made_send, made_recv,
    right_send, right_recv, last_recv, left_send, left_recv, z_send, z_recv, out_send, out_recv,
):
    blk = lax.axis_index("blk")
    group = lax.axis_index("group")
    z_hi, y, core = blk // 16, (blk // 2) % 8, blk % 2
    x, z_lo = group // 2, group % 2
    me = group * 2 + core

    def device(z_hi_at, y_at, core_at, group_at):
        return ((z_hi_at * 8 + y_at) * 2 + core_at, group_at)

    def member(n, way):
        return ((x + way * (n // 2) + XN) % XN) * 2 + (z_lo + n % 2) % 2

    def remote(src, dst, send, recv, to):
        return pltpu.make_async_remote_copy(
            src_ref=src, dst_ref=dst, send_sem=send, recv_sem=recv,
            device_id=to, device_id_type=MESH,
        )

    def each(stop, do):
        def step(n, _):
            do(n)
            return 0

        lax.fori_loop(1, stop, step, 0)

    right = device(z_hi, (y + 1) % 8, core, group)
    left = device(z_hi, (y + 7) % 8, core, group)
    sibling = device(z_hi, y, 1 - core, group)

    loads = [
        pltpu.make_async_copy(there, here, load.at[i])
        for i, (there, here) in enumerate(
            [(act_hbm, act_ref), (grad_hbm, grad_ref), (back_hbm, back_ref)]
        )
    ]
    for copy in loads:
        copy.start()

    barrier = pltpu.get_barrier_semaphore()

    def greet(to):
        pl.semaphore_signal(barrier, inc=1, device_id=to, device_id_type=MESH)

    greet(sibling)
    each(SLICES, lambda n: greet(device(z_hi, y, core, member(n, 1))))
    greet(right)
    greet(left)
    each(ZH, lambda k: greet(device((z_hi + k) % 4, y, core, group)))

    index_work(count_ref, rows_ref, cols_ref, tiles_ref, table_made, code_ref)
    table = pltpu.make_async_copy(table_made, table_ref, load.at[3])
    table.start()
    loads[0].wait()

    def turn(r, _):
        act_t[r] = act_ref[:, pl.ds(pl.multiple_of(r * TILE, TILE), TILE)].T
        return 0

    lax.fori_loop(0, act_ref.shape[1] // TILE, turn, 0, unroll=4)

    loads[1].wait()

    def part(r, _):
        grad_t[r] = grad_ref[:, pl.ds(pl.multiple_of(r * TILE, TILE), TILE)]
        return 0

    lax.fori_loop(0, grad_ref.shape[1] // TILE, part, 0, unroll=4)

    def plane(k):
        return (z_hi + 1 + k) % 4

    def pair(p):
        return (y + 4 - p) % 8, (y + 5 + p) % 8

    def make(m):
        k, p = ORDER[m]

        def tile(core_to, o, j):
            e = (plane(k) * 2 + core_to) * PER_CHUNK + pair(p)[o] * SLOT + j
            r = jnp.clip(table_ref[0, e], 0, act_t.shape[0] - 1)
            c = jnp.clip(table_ref[1, e], 0, grad_t.shape[0] - 1)
            a, b = act_t[r], grad_t[c]
            product = jnp.dot(a, b, preferred_element_type=F32).astype(BF16)
            return product.reshape(SLICES, ROWS, TILE)

        for o in range(2):
            for j in range(SLOT):
                other[m, :, o * SLOT + j] = tile(1 - core, o, j)
        for o in range(2):
            for j in range(SLOT):
                made[m, :, core, o * SLOT + j] = tile(core, o, j)

    def code_swap(way):
        there = codes.at[group, core if way == 1 else 1 - core]
        return remote(code_ref.at[1 - core], there, code_send.at[0], code_recv.at[0], sibling)

    def code_copy(n):
        mine = codes.at[group]
        to = device(z_hi, y, core, member(n, 1))
        return remote(mine, mine, code_send.at[1], code_recv.at[1], to)

    def swap(m, way):
        there = made.at[m, :, core if way == 1 else 1 - core]
        return remote(other.at[m], there, swap_send.at[0], swap_recv.at[m], sibling)

    def made_copy(m, n, part, semaphore):
        g = member(n, 1)
        src, dst = made.at[(m, g, *part)], got.at[(m, group, *part)]
        to = device(z_hi, y, core, g)
        return remote(src, dst, made_send.at[0], made_recv.at[semaphore], to)

    def all_of(ref, semaphore):
        pltpu.make_async_copy(ref, ref, semaphore).wait()

    def right_copy(k, s):
        return remote(
            to_right.at[k, s], from_left.at[k, s], right_send.at[0], right_recv.at[k, s], right
        )

    def left_copy(k, s):
        return remote(
            to_left.at[k, s], from_right.at[k, s], left_send.at[0], left_recv.at[k, s], left
        )

    def z_copy(k):
        to = device(plane(k), y, core, group)
        return remote(to_z.at[k], from_z.at[k], z_send.at[0], z_recv.at[k], to)

    def out_copy(h, n):
        there = out_ref.at[h, group]
        to = device(z_hi, y, core, member(n, 1))
        return remote(there, there, out_send.at[0], out_recv.at[h], to)

    def last_copy(h):
        at = (ZH - 1, 3, slice(h * HALF, (h + 1) * HALF))
        return remote(
            to_right.at[at], from_left.at[at], right_send.at[0], last_recv.at[h], right
        )

    def send(m):
        swap(m, -1).wait_recv()
        if m == 0:
            each(SLICES, lambda n: made_copy(m, n, (1 - core,), m).start())
        elif m < PARTS - 1:
            each(SLICES, lambda n: made_copy(m, n, (), m).start())
        else:
            for o in range(2):
                part = (slice(None), slice(o * SLOT, (o + 1) * SLOT))
                each(SLICES, lambda n, o=o, part=part: made_copy(m, n, part, m + o).start())

    lane = lax.broadcasted_iota(jnp.int32, (YN, TILE), 1)
    row = lax.broadcasted_iota(jnp.int32, (PIECE, CLUSTER * SLOT * ROWS), 0).astype(F32)

    def line_up(k):
        for kk in range(4):
            key = jnp.zeros((YN, TILE), F32)
            for i in range(4):
                turned = pltpu.roll(codes[kk * 2 + i // 2, i % 2], (i + 4 - plane(k)) % 4 * 32, 1)
                key = jnp.where(lane // 32 == i, turned, key)
            keys[k, :, kk * TILE : (kk + 1) * TILE] = key

    def owner_sum(m, o, rows=slice(None)):
        k, p = ORDER[m]
        pick = jnp.where(row[rows] == keys[k, pl.ds(pair(p)[o], 1), :], 1.0, 0.0).astype(BF16)
        parts = got[m, :, :, o * SLOT : (o + 1) * SLOT].reshape(CLUSTER * SLOT * ROWS, TILE)
        return jnp.dot(pick, parts, preferred_element_type=F32)

    def finish(k):
        left_copy(k, 2).wait_recv()
        right_copy(k, 3).wait_recv()
        total = own[k] + from_right[k, 2].astype(F32) + from_left[k, 3].astype(F32)
        to_z[k] = total.astype(BF16)
        z_copy(k).start()

    table.wait()
    make(0)
    pl.semaphore_wait(barrier, 1 + SLICES - 1 + 2 + ZH - 1)
    swap(0, 1).start()
    each(SLICES, lambda n: made_copy(0, n, (core,), 0).start())
    code_swap(1).start()
    codes[group, core] = code_ref[core]
    for m in range(1, AHEAD + 1):
        make(m)
        swap(m, 1).start()
        send(m - 1)
        if m == 1:
            code_swap(-1).wait_recv()
            each(SLICES, lambda n: code_copy(n).start())
    all_of(codes.at[1:], code_recv.at[1])
    for k in range(ZH):
        line_up(k)

    for m in range(PARTS - 1):
        k, p = ORDER[m]
        if m + AHEAD + 1 < PARTS:
            make(m + AHEAD + 1)
            swap(m + AHEAD + 1, 1).start()
        if m + AHEAD < PARTS:
            send(m + AHEAD)
        got[m, group] = made[m, group]
        all_of(got.at[m, 1:], made_recv.at[m])
        rightward = owner_sum(m, 0)
        if p > 0:
            right_copy(k, p - 1).wait_recv()
            rightward += from_left[k, p - 1].astype(F32)
        to_right[k, p] = rightward.astype(BF16)
        right_copy(k, p).start()
        leftward = owner_sum(m, 1)
        if p < 3:
            if p > 0:
                left_copy(k, p - 1).wait_recv()
                leftward += from_right[k, p - 1].astype(F32)
            to_left[k, p] = leftward.astype(BF16)
            left_copy(k, p).start()
        else:
            own[k] = leftward
        if m > 0 and ORDER[m - 1][1] == 3:
            finish(ORDER[m - 1][0])
    m, k = PARTS - 1, ZH - 1
    got[m, group] = made[m, group]
    all_of(got.at[m, 1:, :, :SLOT], made_recv.at[m])
    right_copy(k, 2).wait_recv()
    for h in range(2):
        rows = slice(h * HALF, (h + 1) * HALF)
        rightward = owner_sum(m, 0, rows) + from_left[k, 2, rows].astype(F32)
        to_right[k, 3, rows] = rightward.astype(BF16)
        last_copy(h).start()
    all_of(got.at[m, 1:, :, SLOT:], made_recv.at[m + 1])
    total = owner_sum(m, 1)
    left_copy(k, 2).wait_recv()
    total += from_right[k, 2].astype(F32)
    loads[2].wait()
    mine = pl.ds(pl.multiple_of(group * ROWS, ROWS), ROWS)
    total += back_ref[:, mine, :].astype(F32).reshape(PIECE, TILE)
    for z in range(ZH - 1):
        z_copy(z).wait_recv()
        total += from_z[z].astype(F32)
    own[k] = total
    for h in range(2):
        rows = slice(h * HALF, (h + 1) * HALF)
        last_copy(h).wait_recv()
        total = own[k, rows] + from_left[k, 3, rows].astype(F32)
        out_ref[h, group] = total.astype(BF16).reshape(OWNED // 2, ROWS, TILE)
        for n in FAR_FIRST:
            out_copy(h, n).start()
    for h in range(2):
        all_of(out_ref.at[h, 1:], out_recv.at[h])

    code_swap(1).wait_send()
    all_of(codes.at[1:], code_send.at[1])
    all_of(other, swap_send.at[0])
    all_of(made.at[: PARTS * (SLICES - 1) // SLICES], made_send.at[0])
    all_of(to_right, right_send.at[0])
    all_of(to_left, left_send.at[0])
    all_of(to_z, z_send.at[0])
    all_of(out_ref.at[:, 1:], out_send.at[0])


def split_kernel(mask_ref, summed_ref, update_ref, feedback_ref):
    tiles = update_ref.shape[0]
    for t in range(tiles):
        applied = mask_ref[pl.program_id(0) * tiles + t] == 1
        for g in range(SLICES):
            summed = summed_ref[0, g, t].astype(F32)
            at = slice(g * ROWS, (g + 1) * ROWS)
            update_ref[t, at] = jnp.where(applied, summed, 0.0).astype(BF16)
            feedback_ref[t, at] = jnp.where(applied, 0.0, summed).astype(BF16)


def on_device(
    activations, grad_out, kept_rows, kept_cols, kept_count, owner_tiles, apply_mask, feedback_in
):
    vmem = pl.BlockSpec(memory_space=pltpu.VMEM)
    smem = pl.BlockSpec(memory_space=pltpu.SMEM)
    anywhere = pl.BlockSpec(memory_space=pl.ANY)
    dma = pltpu.SemaphoreType.DMA
    summed = pl.pallas_call(
        main_kernel,
        out_shape=jax.ShapeDtypeStruct((2, SLICES, OWNED // 2, ROWS, TILE), BF16),
        in_specs=[smem, vmem, vmem, vmem, anywhere, anywhere, anywhere],
        out_specs=vmem,
        scratch_shapes=[
            pltpu.VMEM(activations.shape, BF16),
            pltpu.VMEM(grad_out.shape, BF16),
            pltpu.VMEM(feedback_in.shape, BF16),
            pltpu.VMEM((2, TILE), jnp.int32),
            pltpu.SMEM((2, TILE), jnp.int32),
            pltpu.VMEM((CORES, YN, TILE), F32),
            pltpu.VMEM((activations.shape[1] // TILE, TILE, TILE), BF16),
            pltpu.VMEM((grad_out.shape[1] // TILE, TILE, TILE), BF16),
            pltpu.VMEM((PARTS, SLICES, 2 * SLOT, ROWS, TILE), BF16),
            pltpu.VMEM((PARTS, SLICES, CORES, 2 * SLOT, ROWS, TILE), BF16),
            pltpu.VMEM((PARTS, SLICES, CORES, 2 * SLOT, ROWS, TILE), BF16),
            pltpu.VMEM((SLICES, CORES, YN, TILE), F32),
            pltpu.VMEM((ZH, YN, CLUSTER * SLOT * ROWS), F32),
            pltpu.VMEM((ZH, PIECE, TILE), F32),
            pltpu.VMEM((ZH, 4, PIECE, TILE), BF16),
            pltpu.VMEM((ZH, 4, PIECE, TILE), BF16),
            pltpu.VMEM((ZH, 3, PIECE, TILE), BF16),
            pltpu.VMEM((ZH, 3, PIECE, TILE), BF16),
            pltpu.VMEM((ZH - 1, PIECE, TILE), BF16),
            pltpu.VMEM((ZH - 1, PIECE, TILE), BF16),
            dma((4,)),
            dma((2,)), dma((2,)),
            dma((1,)), dma((PARTS,)),
            dma((1,)), dma((PARTS + 1,)),
            dma((1,)), dma((ZH, 4)), dma((2,)),
            dma((1,)), dma((ZH, 3)),
            dma((1,)), dma((ZH - 1,)),
            dma((1,)), dma((2,)),
        ],
        compiler_params=pltpu.CompilerParams(
            collective_id=0, has_side_effects=True, vmem_limit_bytes=56 * 2**20
        ),
    )(
        kept_count, kept_rows, kept_cols, owner_tiles.reshape(-1, TILE),
        activations, grad_out, feedback_in,
    )
    half = pl.BlockSpec((OWNED // 2, TILE, TILE), lambda i: (i, 0, 0))
    pieces = pl.BlockSpec((1, SLICES, OWNED // 2, ROWS, TILE), lambda i: (i, 0, 0, 0, 0))
    return tuple(
        pl.pallas_call(
            split_kernel,
            grid=(2,),
            out_shape=(jax.ShapeDtypeStruct(feedback_in.shape, BF16),) * 2,
            in_specs=[smem, pieces],
            out_specs=(half, half),
        )(apply_mask, summed)
    )


def solution(mesh):
    return jax.shard_map(
        on_device,
        mesh=mesh,
        in_specs=(
            P(("blk", "group"), None),
            P(("blk", "group"), None),
            P(("blk", "group"), None),
            P(("blk", "group"), None),
            P(("blk", "group")),
            P(),
            P("blk"),
            P("blk", None, None),
        ),
        out_specs=(P("blk", None, None), P("blk", None, None)),
        check_vma=False,
    )
```

```python
import functools

import jax
import jax.numpy as jnp
from jax import lax
from jax.experimental import pallas as pl
from jax.experimental.pallas import tpu as pltpu
from jax.sharding import PartitionSpec as P

ZH, YN, CORES, XN, ZL = 4, 8, 2, 4, 2
SLICES = XN * ZL
CLUSTER = SLICES * CORES
SLOT = 2
TILE = 128
ROWS = TILE // SLICES
OWNED = 20
PIECE = OWNED * ROWS
PER_CHUNK = YN * SLOT
PARTS = 16
AHEAD = 11
ORDER = (
    (0, 0), (1, 0), (2, 0), (0, 1), (1, 1), (2, 1), (0, 2), (1, 2),
    (3, 0), (2, 2), (0, 3), (3, 1), (2, 3), (1, 3), (3, 2), (3, 3),
)
FAR_FIRST = (4, 5, 2, 6, 3, 7, 1)
HALF = PIECE // 2
MESH = pl.DeviceIdType.MESH
F32 = jnp.float32
BF16 = jnp.bfloat16


def index_work(count_ref, rows_ref, cols_ref, tiles_ref, table_ref, code_ref):
    n = TILE
    sub = lax.broadcasted_iota(jnp.int32, (n, n), 0).astype(F32)
    lane = lax.broadcasted_iota(jnp.int32, (n, n), 1).astype(F32)
    count = count_ref[0].astype(F32)
    row_of = jnp.broadcast_to(rows_ref[...].astype(F32), (n, n)).T
    col_of = jnp.broadcast_to(cols_ref[...].astype(F32), (n, n)).T
    tile_of = row_of * 64.0 + col_of
    found = jnp.zeros((n, n), F32)
    for k in range(tiles_ref.shape[0]):
        known = tiles_ref[k : k + 1, :].astype(F32)
        found += jnp.where(tile_of == known, lane + 128.0 * k, 0.0)
    position = jnp.broadcast_to(jnp.sum(found, axis=1, keepdims=True), (n, n))
    owner = jnp.floor((position + 0.5) * (1.0 / OWNED))
    label = position - OWNED * owner
    same = (owner.T == owner) & (lane < sub) & (lane < count)
    rank = jnp.sum(jnp.where(same, 1.0, 0.0), axis=1, keepdims=True)
    z_hi = jnp.floor((owner + 0.5) * (1.0 / 16.0))
    in_plane = owner - 16.0 * z_hi
    y = jnp.floor((in_plane + 0.5) * 0.5)
    core = in_plane - 2.0 * y
    slot = ((z_hi * 2.0 + core) * 8.0 + y) * 2.0 + rank
    chosen = (slot == lane) & (sub < count)
    slot_row = jnp.sum(jnp.where(chosen, row_of, 0.0), axis=0, keepdims=True)
    slot_col = jnp.sum(jnp.where(chosen, col_of, 0.0), axis=0, keepdims=True)
    slot_label = jnp.sum(jnp.where(chosen, label + 1.0, 0.0), axis=0, keepdims=True) - 1.0
    table_ref[0:1, :] = slot_row.astype(jnp.int32)
    table_ref[1:2, :] = slot_col.astype(jnp.int32)
    m = CORES * YN
    at = lax.broadcasted_iota(jnp.int32, (m, n), 0)
    s = lax.broadcasted_iota(jnp.int32, (m, n), 1)
    mine = (s // 16) % 2 * 8 + (s // 2) % 8 == at
    spread = jnp.where(mine, jnp.broadcast_to(slot_label, (m, n)), 0.0).astype(BF16)
    s2 = lax.broadcasted_iota(jnp.int32, (n, n), 0)
    l2 = lax.broadcasted_iota(jnp.int32, (n, n), 1)
    pick = jnp.where((s2 // 32 == l2 // 32) & (s2 % 2 == l2 // 16 % 2), 1.0, 0.0).astype(BF16)
    coded = jnp.dot(spread, pick, preferred_element_type=F32) * 16.0
    coded += (lax.broadcasted_iota(jnp.int32, (m, n), 1) % 16).astype(F32)
    code_ref[...] = coded.reshape(CORES, YN, n)


def main_kernel(
    count_ref, rows_ref, cols_ref, tiles_ref, act_hbm, grad_hbm, back_hbm, out_ref,
    act_ref, grad_ref, back_ref, table_made, table_ref, code_ref,
    act_t, grad_t, other, made, got, codes, keys, own,
    to_right, from_left, to_left, from_right, to_z, from_z,
    load, code_send, code_recv, swap_send, swap_recv, made_send, made_recv,
    right_send, right_recv, last_recv, left_send, left_recv, z_send, z_recv, out_send, out_recv,
):
    blk = lax.axis_index("blk")
    group = lax.axis_index("group")
    z_hi, y, core = blk // 16, (blk // 2) % 8, blk % 2
    x, z_lo = group // 2, group % 2
    me = group * 2 + core

    def device(z_hi_at, y_at, core_at, group_at):
        return ((z_hi_at * 8 + y_at) * 2 + core_at, group_at)

    def member(n, way):
        return ((x + way * (n // 2) + XN) % XN) * 2 + (z_lo + n % 2) % 2

    def remote(src, dst, send, recv, to):
        return pltpu.make_async_remote_copy(
            src_ref=src, dst_ref=dst, send_sem=send, recv_sem=recv,
            device_id=to, device_id_type=MESH,
        )

    def each(stop, do):
        def step(n, _):
            do(n)
            return 0

        lax.fori_loop(1, stop, step, 0)

    right = device(z_hi, (y + 1) % 8, core, group)
    left = device(z_hi, (y + 7) % 8, core, group)
    sibling = device(z_hi, y, 1 - core, group)

    loads = [
        pltpu.make_async_copy(there, here, load.at[i])
        for i, (there, here) in enumerate(
            [(act_hbm, act_ref), (grad_hbm, grad_ref), (back_hbm, back_ref)]
        )
    ]
    for copy in loads:
        copy.start()

    barrier = pltpu.get_barrier_semaphore()

    def greet(to):
        pl.semaphore_signal(barrier, inc=1, device_id=to, device_id_type=MESH)

    greet(sibling)
    each(SLICES, lambda n: greet(device(z_hi, y, core, member(n, 1))))
    greet(right)
    greet(left)
    each(ZH, lambda k: greet(device((z_hi + k) % 4, y, core, group)))

    index_work(count_ref, rows_ref, cols_ref, tiles_ref, table_made, code_ref)
    table = pltpu.make_async_copy(table_made, table_ref, load.at[3])
    table.start()
    loads[0].wait()

    def turn(r, _):
        act_t[r] = act_ref[:, pl.ds(pl.multiple_of(r * TILE, TILE), TILE)].T
        return 0

    lax.fori_loop(0, act_ref.shape[1] // TILE, turn, 0, unroll=4)

    loads[1].wait()

    def part(r, _):
        grad_t[r] = grad_ref[:, pl.ds(pl.multiple_of(r * TILE, TILE), TILE)]
        return 0

    lax.fori_loop(0, grad_ref.shape[1] // TILE, part, 0, unroll=4)

    def plane(k):
        return (z_hi + 1 + k) % 4

    def pair(p):
        return (y + 4 - p) % 8, (y + 5 + p) % 8

    def make(m):
        k, p = ORDER[m]

        def tile(core_to, o, j):
            e = (plane(k) * 2 + core_to) * PER_CHUNK + pair(p)[o] * SLOT + j
            r = jnp.clip(table_ref[0, e], 0, act_t.shape[0] - 1)
            c = jnp.clip(table_ref[1, e], 0, grad_t.shape[0] - 1)
            a, b = act_t[r], grad_t[c]
            product = jnp.dot(a, b, preferred_element_type=F32).astype(BF16)
            return product.reshape(SLICES, ROWS, TILE)

        for o in range(2):
            for j in range(SLOT):
                other[m, :, o * SLOT + j] = tile(1 - core, o, j)
        for o in range(2):
            for j in range(SLOT):
                made[m, :, core, o * SLOT + j] = tile(core, o, j)

    def code_swap(way):
        there = codes.at[group, core if way == 1 else 1 - core]
        return remote(code_ref.at[1 - core], there, code_send.at[0], code_recv.at[0], sibling)

    def code_copy(n):
        mine = codes.at[group]
        to = device(z_hi, y, core, member(n, 1))
        return remote(mine, mine, code_send.at[1], code_recv.at[1], to)

    def swap(m, way):
        there = made.at[m, :, core if way == 1 else 1 - core]
        return remote(other.at[m], there, swap_send.at[0], swap_recv.at[m], sibling)

    def made_copy(m, n, part, semaphore):
        g = member(n, 1)
        src, dst = made.at[(m, g, *part)], got.at[(m, group, *part)]
        to = device(z_hi, y, core, g)
        return remote(src, dst, made_send.at[0], made_recv.at[semaphore], to)

    def all_of(ref, semaphore):
        pltpu.make_async_copy(ref, ref, semaphore).wait()

    def right_copy(k, s):
        return remote(
            to_right.at[k, s], from_left.at[k, s], right_send.at[0], right_recv.at[k, s], right
        )

    def left_copy(k, s):
        return remote(
            to_left.at[k, s], from_right.at[k, s], left_send.at[0], left_recv.at[k, s], left
        )

    def z_copy(k):
        to = device(plane(k), y, core, group)
        return remote(to_z.at[k], from_z.at[k], z_send.at[0], z_recv.at[k], to)

    def out_copy(h, n):
        there = out_ref.at[h, group]
        to = device(z_hi, y, core, member(n, 1))
        return remote(there, there, out_send.at[0], out_recv.at[h], to)

    def last_copy(h):
        at = (ZH - 1, 3, slice(h * HALF, (h + 1) * HALF))
        return remote(
            to_right.at[at], from_left.at[at], right_send.at[0], last_recv.at[h], right
        )

    def send(m):
        swap(m, -1).wait_recv()
        if m < PARTS - 1:
            each(SLICES, lambda n: made_copy(m, n, (1 - core,), m).start())
        else:
            for o in range(2):
                part = (slice(None), slice(o * SLOT, (o + 1) * SLOT))
                each(SLICES, lambda n, o=o, part=part: made_copy(m, n, part, m + o).start())

    lane = lax.broadcasted_iota(jnp.int32, (YN, TILE), 1)
    row = lax.broadcasted_iota(jnp.int32, (PIECE, CLUSTER * SLOT * ROWS), 0).astype(F32)

    def line_up(k):
        for kk in range(4):
            key = jnp.zeros((YN, TILE), F32)
            for i in range(4):
                turned = pltpu.roll(codes[kk * 2 + i // 2, i % 2], (i + 4 - plane(k)) % 4 * 32, 1)
                key = jnp.where(lane // 32 == i, turned, key)
            keys[k, :, kk * TILE : (kk + 1) * TILE] = key

    def send_own(m):
        if m < PARTS - 1:
            each(SLICES, lambda n: made_copy(m, n, (core,), m).start())

    def owner_sum(m, o, rows=slice(None)):
        k, p = ORDER[m]
        pick = jnp.where(row[rows] == keys[k, pl.ds(pair(p)[o], 1), :], 1.0, 0.0).astype(BF16)
        parts = got[m, :, :, o * SLOT : (o + 1) * SLOT].reshape(CLUSTER * SLOT * ROWS, TILE)
        return jnp.dot(pick, parts, preferred_element_type=F32)

    def finish(k):
        left_copy(k, 2).wait_recv()
        right_copy(k, 3).wait_recv()
        total = own[k] + from_right[k, 2].astype(F32) + from_left[k, 3].astype(F32)
        to_z[k] = total.astype(BF16)
        z_copy(k).start()

    table.wait()
    make(0)
    pl.semaphore_wait(barrier, 1 + SLICES - 1 + 2 + ZH - 1)
    swap(0, 1).start()
    send_own(0)
    code_swap(1).start()
    codes[group, core] = code_ref[core]
    for m in range(1, AHEAD + 1):
        make(m)
        swap(m, 1).start()
        send_own(m)
        send(m - 1)
        if m == 1:
            code_swap(-1).wait_recv()
            each(SLICES, lambda n: code_copy(n).start())
    all_of(codes.at[1:], code_recv.at[1])
    for k in range(ZH):
        line_up(k)

    for m in range(PARTS - 1):
        k, p = ORDER[m]
        if m + AHEAD + 1 < PARTS:
            make(m + AHEAD + 1)
            swap(m + AHEAD + 1, 1).start()
            send_own(m + AHEAD + 1)
        if m + AHEAD < PARTS:
            send(m + AHEAD)
        got[m, group] = made[m, group]
        all_of(got.at[m, 1:], made_recv.at[m])
        rightward = owner_sum(m, 0)
        if p > 0:
            right_copy(k, p - 1).wait_recv()
            rightward += from_left[k, p - 1].astype(F32)
        to_right[k, p] = rightward.astype(BF16)
        right_copy(k, p).start()
        leftward = owner_sum(m, 1)
        if p < 3:
            if p > 0:
                left_copy(k, p - 1).wait_recv()
                leftward += from_right[k, p - 1].astype(F32)
            to_left[k, p] = leftward.astype(BF16)
            left_copy(k, p).start()
        else:
            own[k] = leftward
        if m > 0 and ORDER[m - 1][1] == 3:
            finish(ORDER[m - 1][0])
    m, k = PARTS - 1, ZH - 1
    got[m, group] = made[m, group]
    all_of(got.at[m, 1:, :, :SLOT], made_recv.at[m])
    right_copy(k, 2).wait_recv()
    for h in range(2):
        rows = slice(h * HALF, (h + 1) * HALF)
        rightward = owner_sum(m, 0, rows) + from_left[k, 2, rows].astype(F32)
        to_right[k, 3, rows] = rightward.astype(BF16)
        last_copy(h).start()
    all_of(got.at[m, 1:, :, SLOT:], made_recv.at[m + 1])
    total = owner_sum(m, 1)
    left_copy(k, 2).wait_recv()
    total += from_right[k, 2].astype(F32)
    loads[2].wait()
    mine = pl.ds(pl.multiple_of(group * ROWS, ROWS), ROWS)
    total += back_ref[:, mine, :].astype(F32).reshape(PIECE, TILE)
    for z in range(ZH - 1):
        z_copy(z).wait_recv()
        total += from_z[z].astype(F32)
    own[k] = total
    for h in range(2):
        rows = slice(h * HALF, (h + 1) * HALF)
        last_copy(h).wait_recv()
        total = own[k, rows] + from_left[k, 3, rows].astype(F32)
        out_ref[h, group] = total.astype(BF16).reshape(OWNED // 2, ROWS, TILE)
        for n in FAR_FIRST:
            out_copy(h, n).start()
    for h in range(2):
        all_of(out_ref.at[h, 1:], out_recv.at[h])

    code_swap(1).wait_send()
    all_of(codes.at[1:], code_send.at[1])
    all_of(other, swap_send.at[0])
    all_of(made.at[: PARTS * (SLICES - 1) // SLICES], made_send.at[0])
    all_of(to_right, right_send.at[0])
    all_of(to_left, left_send.at[0])
    all_of(to_z, z_send.at[0])
    all_of(out_ref.at[:, 1:], out_send.at[0])


def split_kernel(mask_ref, summed_ref, update_ref, feedback_ref):
    tiles = update_ref.shape[0]
    for t in range(tiles):
        applied = mask_ref[pl.program_id(0) * tiles + t] == 1
        for g in range(SLICES):
            summed = summed_ref[0, g, t].astype(F32)
            at = slice(g * ROWS, (g + 1) * ROWS)
            update_ref[t, at] = jnp.where(applied, summed, 0.0).astype(BF16)
            feedback_ref[t, at] = jnp.where(applied, 0.0, summed).astype(BF16)


def on_device(
    activations, grad_out, kept_rows, kept_cols, kept_count, owner_tiles, apply_mask, feedback_in
):
    vmem = pl.BlockSpec(memory_space=pltpu.VMEM)
    smem = pl.BlockSpec(memory_space=pltpu.SMEM)
    anywhere = pl.BlockSpec(memory_space=pl.ANY)
    dma = pltpu.SemaphoreType.DMA
    summed = pl.pallas_call(
        main_kernel,
        out_shape=jax.ShapeDtypeStruct((2, SLICES, OWNED // 2, ROWS, TILE), BF16),
        in_specs=[smem, vmem, vmem, vmem, anywhere, anywhere, anywhere],
        out_specs=vmem,
        scratch_shapes=[
            pltpu.VMEM(activations.shape, BF16),
            pltpu.VMEM(grad_out.shape, BF16),
            pltpu.VMEM(feedback_in.shape, BF16),
            pltpu.VMEM((2, TILE), jnp.int32),
            pltpu.SMEM((2, TILE), jnp.int32),
            pltpu.VMEM((CORES, YN, TILE), F32),
            pltpu.VMEM((activations.shape[1] // TILE, TILE, TILE), BF16),
            pltpu.VMEM((grad_out.shape[1] // TILE, TILE, TILE), BF16),
            pltpu.VMEM((PARTS, SLICES, 2 * SLOT, ROWS, TILE), BF16),
            pltpu.VMEM((PARTS, SLICES, CORES, 2 * SLOT, ROWS, TILE), BF16),
            pltpu.VMEM((PARTS, SLICES, CORES, 2 * SLOT, ROWS, TILE), BF16),
            pltpu.VMEM((SLICES, CORES, YN, TILE), F32),
            pltpu.VMEM((ZH, YN, CLUSTER * SLOT * ROWS), F32),
            pltpu.VMEM((ZH, PIECE, TILE), F32),
            pltpu.VMEM((ZH, 4, PIECE, TILE), BF16),
            pltpu.VMEM((ZH, 4, PIECE, TILE), BF16),
            pltpu.VMEM((ZH, 3, PIECE, TILE), BF16),
            pltpu.VMEM((ZH, 3, PIECE, TILE), BF16),
            pltpu.VMEM((ZH - 1, PIECE, TILE), BF16),
            pltpu.VMEM((ZH - 1, PIECE, TILE), BF16),
            dma((4,)),
            dma((2,)), dma((2,)),
            dma((1,)), dma((PARTS,)),
            dma((1,)), dma((PARTS + 1,)),
            dma((1,)), dma((ZH, 4)), dma((2,)),
            dma((1,)), dma((ZH, 3)),
            dma((1,)), dma((ZH - 1,)),
            dma((1,)), dma((2,)),
        ],
        compiler_params=pltpu.CompilerParams(
            collective_id=0, has_side_effects=True, vmem_limit_bytes=56 * 2**20
        ),
    )(
        kept_count, kept_rows, kept_cols, owner_tiles.reshape(-1, TILE),
        activations, grad_out, feedback_in,
    )
    half = pl.BlockSpec((OWNED // 2, TILE, TILE), lambda i: (i, 0, 0))
    pieces = pl.BlockSpec((1, SLICES, OWNED // 2, ROWS, TILE), lambda i: (i, 0, 0, 0, 0))
    return tuple(
        pl.pallas_call(
            split_kernel,
            grid=(2,),
            out_shape=(jax.ShapeDtypeStruct(feedback_in.shape, BF16),) * 2,
            in_specs=[smem, pieces],
            out_specs=(half, half),
        )(apply_mask, summed)
    )


def solution(mesh):
    return jax.shard_map(
        on_device,
        mesh=mesh,
        in_specs=(
            P(("blk", "group"), None),
            P(("blk", "group"), None),
            P(("blk", "group"), None),
            P(("blk", "group"), None),
            P(("blk", "group")),
            P(),
            P("blk"),
            P("blk", None, None),
        ),
        out_specs=(P("blk", None, None), P("blk", None, None)),
        check_vma=False,
    )
```
